128 devices in a mesh: dp: 8 (over z_hi, x), tensor: 16 (over y, z_lo, core).
Axes of the slice: x: 4, y: 4, z: 4 (z_hi: 2, z_lo: 2; z = z_hi * 2 + z_lo), core: 2. Of those that a mesh axis runs over, the one named last changes fastest.
Arguments:
- tokens: bfloat16 [2048, 4608], P(('dp', 'tensor')), may hold values from -6 to 6
- tangent: bfloat16 [2048, 4608], P(('dp', 'tensor')), may hold values from -6 to 6
- hessian_weight: float32 [2048], P('dp'), may hold values from 0.02 to 0.2
- gate_weight: bfloat16 [4608, 18432], P(None, 'tensor'), may hold values from -0.09375 to 0.09375
- up_weight: bfloat16 [4608, 18432], P(None, 'tensor'), may hold values from -0.09375 to 0.09375
- down_weight: bfloat16 [18432, 4608], P('tensor', 'dp'), may hold values from -0.046875 to 0.046875
Outputs:
- layer_out: bfloat16 [2048, 4608], P(('dp', 'tensor'))
- out_tangent: bfloat16 [2048, 4608], P(('dp', 'tensor'))
- curvature: bfloat16 [18432, 4608], P('tensor', 'dp')
The draws below stay inside these ranges and needn't reach their ends.
All inputs are finite; a program needn't handle non-finite values.
Results may differ from the reference program's by a relative error of at most 0.03.
Values may be sent and summed in bfloat16 or wider, within the bound.
No kernel may reach another device: no remote copies, remote signals or barrier semaphores. Data moves between devices by JAX's collectives and lax.ppermute only.
A program may use at most 192 MiB of HBM per device.

```python
import math
import jax
import jax.numpy as jnp
from jax import lax

D = 4608
FF = 18432
TOKENS = 2048


def level_of(rng, dims, pieces, low, largest):
    factor_of, own = 1.0, jax.random.fold_in(rng, 6)
    for dim, shards_of in pieces:
        heights = jnp.exp(jax.random.uniform(jax.random.fold_in(own, dim), (shards_of,), jnp.float32, low / len(pieces), largest / len(pieces)))
        factor_of = factor_of * jnp.repeat(heights, dims[dim] // shards_of).reshape([-1 if axis == dim else 1 for axis in range(len(dims))])
    return factor_of


def bell_draw(key, extent, spread, bound, cuts=(), kind=jnp.bfloat16):
    values = spread * jax.random.normal(key, extent, jnp.float32)
    if cuts:
        values = values * level_of(key, extent, cuts, -0.22, 0.18)
    return jnp.clip(values, -bound, bound).astype(kind)


def setup_inputs(seed: int = 0) -> dict:
    splits = jax.random.split(jax.random.key(seed), 7)
    return {
        "tokens": bell_draw(splits[0], (TOKENS, D), 1.0, 6.0, ((0, 128),)),
        "tangent": bell_draw(splits[1], (TOKENS, D), 1.0, 6.0, ((0, 128),)),
        "hessian_weight": jnp.clip(jnp.exp(math.log(0.2) - 2.3025851 * jax.random.uniform(splits[2], (TOKENS,), jnp.float32) ** level_of(splits[2], (TOKENS,), ((0, 8),), -0.2, 0.2)), 0.02, 0.2),
        "gate_weight": bell_draw(splits[3], (D, FF), D ** -0.5, 0.09375, ((1, 16),)),
        "up_weight": bell_draw(splits[4], (D, FF), D ** -0.5, 0.09375, ((1, 16),)),
        "down_weight": bell_draw(splits[5], (FF, D), FF ** -0.5, 0.046875, ((0, 16), (1, 8))),
    }


gelu_scale = 0.7978845608
cubic_coeff = 0.044715


def gelu_pair(values_in):
    inner_arg = gelu_scale * (values_in + cubic_coeff * values_in * values_in * values_in)
    tanh_term = jnp.tanh(inner_arg)
    activated = 0.5 * values_in * (1.0 + tanh_term)
    gelu_slope = 0.5 * (1.0 + tanh_term) + 0.5 * values_in * (1.0 - tanh_term * tanh_term) * gelu_scale * (1.0 + 3.0 * cubic_coeff * values_in * values_in)
    return activated, gelu_slope


def reference(tokens, tangent, hessian_weight, gate_weight, up_weight, down_weight):
    gate_term = jnp.dot(tokens, gate_weight, preferred_element_type=jnp.float32)
    up_term = jnp.dot(tokens, up_weight, preferred_element_type=jnp.float32)
    gate_tan = jnp.dot(tangent, gate_weight, preferred_element_type=jnp.float32)
    up_tan = jnp.dot(tangent, up_weight, preferred_element_type=jnp.float32)
    activated, gelu_slope = gelu_pair(gate_term)
    hidden = (activated * up_term).astype(jnp.bfloat16)
    hidden_tan = (gelu_slope * gate_tan * up_term + activated * up_tan).astype(jnp.bfloat16)
    out_full = jnp.dot(hidden, down_weight, preferred_element_type=jnp.float32)
    tan_full = jnp.dot(hidden_tan, down_weight, preferred_element_type=jnp.float32)
    weighted = (hessian_weight[:, None] * tan_full).astype(jnp.bfloat16)
    curvature = lax.dot_general(hidden, weighted, (((0,), (0,)), ((), ())), preferred_element_type=jnp.float32)
    return out_full.astype(jnp.bfloat16), tan_full.astype(jnp.bfloat16), curvature.astype(jnp.bfloat16)
```

```python
import jax
import jax.numpy as jnp
from jax import lax
from jax.sharding import PartitionSpec as P

gelu_scale = 0.7978845608
cubic_coeff = 0.044715

X, Y = 4, 4


def fetch_t(value, dy=0, dz=0, dc=0):
    pairs = []
    for y in range(Y):
        for z in range(2):
            for c in range(2):
                source = (((y + dy) % Y) * 2 + (z + dz) % 2) * 2 + (c + dc) % 2
                pairs.append((source, (y * 2 + z) * 2 + c))
    return lax.ppermute(value, "tensor", pairs)


def fetch_d(value, dh=0, dx=0):
    pairs = []
    for h in range(2):
        for x in range(X):
            pairs.append((((h + dh) % 2) * X + (x + dx) % X, h * X + x))
    return lax.ppermute(value, "dp", pairs)


def gather8(piece):
    half = piece.shape[0] // 2
    up = fetch_t(piece, dy=1)
    down = fetch_t(piece, dy=-1)
    side = fetch_t(piece, dz=1)
    far_lo = fetch_t(up[:half], dy=1)
    far_hi = fetch_t(down[half:], dy=-1)
    up_side = fetch_t(side, dy=1)
    down_side = fetch_t(side, dy=-1)
    far = jnp.concatenate((far_lo, far_hi))
    far_side = fetch_t(far, dz=1)
    return jnp.stack((piece, side, up, up_side, down, down_side, far, far_side))


def ring_x(value):
    half = value.shape[0] // 2
    right = fetch_d(value, dx=1)
    left = fetch_d(value, dx=-1)
    far_lo = fetch_d(right[:half], dx=1)
    far_hi = fetch_d(left[half:], dx=-1)
    return value, right, jnp.concatenate((far_lo, far_hi)), left


def reduce_tensor(partial):
    rows = partial.shape[0] // 16
    other = fetch_t(partial[8 * rows :].astype(jnp.bfloat16), dc=1)
    chip = partial[: 8 * rows] + other.astype(jnp.float32)
    chip = chip.reshape(4, 2 * rows, -1)
    sent = chip[1:].astype(jnp.bfloat16)
    from_down = fetch_t(sent[0], dy=-1)
    from_up = fetch_t(sent[1], dy=1)
    from_far = fetch_t(sent[2], dy=2)
    column = (
        chip[0]
        + from_down.astype(jnp.float32)
        + from_up.astype(jnp.float32)
        + from_far.astype(jnp.float32)
    )
    from_side = fetch_t(column[rows:].astype(jnp.bfloat16), dz=1)
    return column[:rows] + from_side.astype(jnp.float32)


def gelu_pair(values_in):
    inner_arg = gelu_scale * (values_in + cubic_coeff * values_in * values_in * values_in)
    tanh_term = jnp.tanh(inner_arg)
    activated = 0.5 * values_in * (1.0 + tanh_term)
    gelu_slope = 0.5 * (1.0 + tanh_term) + 0.5 * values_in * (
        1.0 - tanh_term * tanh_term
    ) * gelu_scale * (1.0 + 3.0 * cubic_coeff * values_in * values_in)
    return (activated, gelu_slope)


def hidden_of(pieces, gate_weight, up_weight):
    count, _, rows, width = pieces.shape
    flat = pieces.reshape(count * 2 * rows, width)
    gate = jnp.dot(flat, gate_weight, preferred_element_type=jnp.float32)
    up = jnp.dot(flat, up_weight, preferred_element_type=jnp.float32)
    gate = gate.reshape(count, 2, rows, -1)
    up = up.reshape(count, 2, rows, -1)
    activated, gelu_slope = gelu_pair(gate[:, 0])
    hidden = activated * up[:, 0]
    tangent = gelu_slope * gate[:, 1] * up[:, 0] + activated * up[:, 1]
    return (
        hidden.astype(jnp.bfloat16).reshape(count * rows, -1),
        tangent.astype(jnp.bfloat16).reshape(count * rows, -1),
    )


def product(left, right):
    return jnp.dot(left, right, preferred_element_type=jnp.float32)


def whole_rows(own, other, place_h, place_x):
    width = own.shape[1]
    block = width // X

    def turned(part):
        twice = jnp.concatenate((part, part), axis=1)
        return lax.dynamic_slice_in_dim(twice, ((X - place_x) % X) * block, width, 1)

    own, other = turned(own), turned(other)
    first = place_h == 0
    return jnp.concatenate((jnp.where(first, own, other), jnp.where(first, other, own)), axis=1)


def shards(tokens, tangent, hessian_weight, gate_weight, up_weight, down_weight):
    rows, width = tokens.shape
    place_d = lax.axis_index("dp")
    place_t = lax.axis_index("tensor")
    place_h, place_x = place_d // X, place_d % X

    pieces_own = gather8(jnp.stack((tokens, tangent)))
    pieces_other = fetch_t(pieces_own, dc=1)

    blocks = ring_x(down_weight)
    down_half = jnp.concatenate(blocks, axis=1)

    weight_rows = lax.dynamic_slice_in_dim(hessian_weight, place_t * rows, rows, 0)
    weight_rows = weight_rows.reshape(1, rows)
    weight_other = fetch_d(weight_rows, dh=1)

    hid_a, tan_a = hidden_of(pieces_own, gate_weight, up_weight)
    tan_a1 = fetch_d(tan_a, dh=1)
    hid_b, tan_b = hidden_of(pieces_other, gate_weight, up_weight)
    tan_b1 = fetch_d(tan_b, dh=1)
    hid_0 = jnp.concatenate((hid_a, hid_b))
    tan_0 = jnp.concatenate((tan_a, tan_b))
    tan_1 = jnp.concatenate((tan_a1, tan_b1))
    hid_1 = fetch_d(hid_0, dh=1)

    tan_rows_0 = reduce_tensor(product(tan_0, down_half))
    tan_rows_1 = reduce_tensor(product(tan_1, down_half))

    weighted = jnp.stack(
        (weight_rows[0][:, None] * tan_rows_0, weight_other[0][:, None] * tan_rows_1)
    ).astype(jnp.bfloat16)
    block = down_weight.shape[1]
    parts = [weighted[..., :block]]
    for k in range(1, X):
        send = weighted[..., ((X - k) % X) * block : ((X - k) % X + 1) * block]
        parts.append(fetch_d(send, dx=k))
    piece = jnp.stack(parts)
    near = gather8(piece)
    far = fetch_t(near, dc=1)
    weighted_all = jnp.stack((near, far)).reshape(16, X, 2, rows, block)
    weighted_all = weighted_all.transpose(1, 2, 0, 3, 4).reshape(-1, block)

    hid_x = ring_x(jnp.stack((hid_0, hid_1)))
    hidden_all = jnp.stack(hid_x).reshape(-1, hid_0.shape[1])
    curvature = lax.dot_general(
        hidden_all, weighted_all, (((0,), (0,)), ((), ())), preferred_element_type=jnp.float32
    ).astype(jnp.bfloat16)

    out_rows_0 = reduce_tensor(product(hid_0, down_half))
    out_rows_1 = reduce_tensor(product(hid_1, down_half))

    tan_other = fetch_d(tan_rows_1.astype(jnp.bfloat16), dh=1)
    out_other = fetch_d(out_rows_1.astype(jnp.bfloat16), dh=1)
    layer_out = whole_rows(out_rows_0.astype(jnp.bfloat16), out_other, place_h, place_x)
    out_tangent = whole_rows(tan_rows_0.astype(jnp.bfloat16), tan_other, place_h, place_x)
    return layer_out, out_tangent, curvature


def solution(mesh):
    placed = (
        P(("dp", "tensor"), None),
        P(("dp", "tensor"), None),
        P("dp"),
        P(None, "tensor"),
        P(None, "tensor"),
        P("tensor", "dp"),
    )
    return jax.shard_map(
        shards,
        mesh=mesh,
        in_specs=placed,
        out_specs=(P(("dp", "tensor"), None), P(("dp", "tensor"), None), P("tensor", "dp")),
        check_vma=False,
    )
```

```python
import jax
import jax.numpy as jnp
from jax import lax
from jax.experimental import pallas as pl
from jax.experimental.pallas import tpu as pltpu
from jax.sharding import PartitionSpec as P

gelu_scale = 0.7978845608
cubic_coeff = 0.044715


def fetch_t(value, ky=0, kz=0, kc=0):
    key = ky * 4 + kz * 2 + kc
    return lax.ppermute(value, "tensor", [(i ^ key, i) for i in range(16)])


def fetch_d(value, kh=0, kx=0):
    key = kh * 4 + kx
    return lax.ppermute(value, "dp", [(i ^ key, i) for i in range(8)])


def after(value, *done):
    def nothing(*refs):
        del refs

    anywhere = pl.BlockSpec(memory_space=pl.ANY)
    return pl.pallas_call(
        nothing,
        out_shape=jax.ShapeDtypeStruct(value.shape, value.dtype),
        in_specs=[anywhere] * (1 + len(done)),
        out_specs=anywhere,
        input_output_aliases={0: 0},
        compiler_params=pltpu.CompilerParams(vmem_limit_bytes=1 << 17),
    )(value, *done)


def exchange_x(value):
    return fetch_d(value, kx=1), fetch_d(value, kx=3)


def far_x(one, three):
    half = one.shape[0] // 2
    return fetch_d(three[:half], kx=1), fetch_d(one[half:], kx=3)


def gather_y(pair):
    one = fetch_t(pair, ky=1)
    three = fetch_t(pair, ky=3)
    return one, three, (fetch_t(three[:1], ky=1), fetch_t(one[1:], ky=3))


def core_sum(partial):
    other = fetch_t(partial[:, 1], kc=1)
    return partial[:, 0].astype(jnp.float32) + other.astype(jnp.float32)


def column_sum(chip, ready=()):
    column = after(chip[:, 0], *ready) if ready else chip[:, 0]
    for key, place in ((2, 3), (1, 1), (3, 2)):
        got = fetch_t(chip[:, place].astype(jnp.bfloat16), ky=key)
        column = column + got.astype(jnp.float32)
    return column


def side_sum(column):
    send = jnp.concatenate((column[:, 1], column[:1, 0])).astype(jnp.bfloat16)
    got = fetch_t(send, kz=1).astype(jnp.float32)
    return column[:, 0] + got[:-1], column[0, 1] + got[-1]


def gelu_pair(values_in):
    inner_arg = gelu_scale * (values_in + cubic_coeff * values_in * values_in * values_in)
    tanh_term = jnp.tanh(inner_arg)
    activated = 0.5 * values_in * (1.0 + tanh_term)
    gelu_slope = 0.5 * (1.0 + tanh_term) + 0.5 * values_in * (
        1.0 - tanh_term * tanh_term
    ) * gelu_scale * (1.0 + 3.0 * cubic_coeff * values_in * values_in)
    return (activated, gelu_slope)


def gate_of(own, other, gate_weight):
    flat = jnp.concatenate((*own, *other))
    flat = flat.reshape(-1, flat.shape[-1])
    return flat, jnp.dot(flat, gate_weight, preferred_element_type=jnp.float32)


def hidden_of(flat, gate, up_weight, rows):
    up = jnp.dot(flat, up_weight, preferred_element_type=jnp.float32)
    gate = gate.reshape(-1, 2, rows, gate.shape[1])
    up = up.reshape(-1, 2, rows, up.shape[1])
    activated, gelu_slope = gelu_pair(gate[:, 0])
    hidden = activated * up[:, 0]
    tangent = gelu_slope * gate[:, 1] * up[:, 0] + activated * up[:, 1]
    both = jnp.stack((tangent.astype(jnp.bfloat16), hidden.astype(jnp.bfloat16)))
    return both.reshape(2, 2, -1, gate.shape[-1])


def product(left, blocks, rows):
    groups = left.shape[0]
    left = left.reshape(-1, left.shape[-1])
    height, depth = left.shape
    columns = sum(block.shape[0] for block in blocks)
    tile = 256 if columns % 256 == 0 else columns
    n_block = len(blocks)

    def kernel(left_ref, *refs):
        out_ref, right_ref, sems = refs[-3:]
        copies, place = [], 0
        for k, block in enumerate(refs[:n_block]):
            size = block.shape[0]
            copy = pltpu.make_async_copy(block, right_ref.at[pl.ds(place, size)], sems.at[k])
            copy.start()
            copies.append((place, copy))
            place += size
        for at in range(0, columns, tile):
            while copies and copies[0][0] < at + tile:
                copies.pop(0)[1].wait()
            total = lax.dot_general(
                left_ref[...],
                right_ref[at : at + tile, :],
                (((1,), (1,)), ((), ())),
                preferred_element_type=jnp.float32,
            )
            out_ref[:, at : at + tile] = total.astype(jnp.bfloat16)

    near = pl.BlockSpec(memory_space=pltpu.VMEM)
    anywhere = pl.BlockSpec(memory_space=pl.ANY)
    out = pl.pallas_call(
        kernel,
        out_shape=jax.ShapeDtypeStruct((height, columns), jnp.bfloat16),
        in_specs=[near] + [anywhere] * n_block,
        out_specs=near,
        scratch_shapes=[
            pltpu.VMEM((columns, depth), jnp.bfloat16),
            pltpu.SemaphoreType.DMA((n_block,)),
        ],
        compiler_params=pltpu.CompilerParams(vmem_limit_bytes=16 << 20),
        cost_estimate=pl.CostEstimate(
            flops=2 * height * depth * columns,
            bytes_accessed=2 * columns * (depth + height),
            transcendentals=0,
        ),
    )(left, *blocks)
    return out.reshape(groups, 2, 4, 2, rows, columns)


def whole_rows(own, other, place_h, place_x):
    block = own.shape[-1] // 4
    both = jnp.stack((own, other))
    b = [both[..., k * block : (k + 1) * block] for k in range(4)]
    odd = place_x & 1 == 1
    one = [jnp.where(odd, b[k ^ 1], b[k]) for k in range(4)]
    high = place_x & 2 == 2
    two = [jnp.where(high, one[k ^ 2], one[k]) for k in range(4)]
    second = place_h == 1
    halves = [[jnp.where(second, t[1 - h], t[h]) for t in two] for h in range(2)]
    return jnp.concatenate(halves[0] + halves[1], axis=-1)


def shards(tokens, tangent, hessian_weight, gate_weight, up_weight, down_weight):
    rows, width = tokens.shape
    place_d = lax.axis_index("dp")
    place_t = lax.axis_index("tensor")
    place_h, place_x = place_d // 4, place_d % 4

    piece = jnp.stack((tokens, tangent))
    pair = jnp.stack((piece, fetch_t(piece, kz=1)))
    pair_other = fetch_t(pair, kc=1)
    one, three, halves = gather_y(pair)
    one_other = fetch_t(one, kc=1)
    three_other = fetch_t(three, kc=1)

    down_0 = after(down_weight.T, piece)
    down_1, down_3 = exchange_x(down_0)
    down_lo, down_hi = far_x(down_1, down_3)
    down_half = (down_0, down_1, down_lo, down_hi, down_3)

    own_rows = jnp.stack(
        [
            lax.dynamic_slice_in_dim(hessian_weight, (place_t ^ key) * rows, rows, 0)
            for key in (0, 2)
        ]
    )
    other_rows = fetch_d(after(own_rows, pair), kh=1)

    pair_other = after(pair_other, other_rows)
    flat, gate = gate_of((pair, one), (pair_other, one_other), gate_weight)
    two = jnp.concatenate([after(half, gate) for half in halves])
    two_other = fetch_t(two, kc=1)
    both_a = hidden_of(after(flat, gate, down_1, down_3), gate, up_weight, rows)
    both_a1 = fetch_d(both_a, kh=1)
    two_other = after(two_other, both_a)
    both_b = hidden_of(
        *gate_of((three, two), (three_other, two_other), gate_weight), up_weight, rows
    )
    both_b1 = fetch_d(both_b, kh=1)
    both_0 = jnp.concatenate((both_a, both_b), axis=2)
    both_1 = jnp.concatenate((both_a1, both_b1), axis=2)

    chip_0 = core_sum(product(after(both_0, both_a1), down_half, rows))
    chip_0 = after(chip_0, both_b1)
    partial_1 = product(both_1, down_half, rows)
    column_0 = column_sum(chip_0, (partial_1,))
    rows_0, side_0 = side_sum(column_0)
    chip_1 = core_sum(partial_1)
    rows_1, side_1 = side_sum(column_sum(chip_1))

    hid_0, hid_1 = both_0[1], both_1[1]
    one_0, three_0 = exchange_x(hid_0)
    lo_0, hi_0 = far_x(after(one_0, chip_1), after(three_0, chip_1))
    one_1, three_1 = exchange_x(after(hid_1, lo_0, hi_0))

    tan_rows = jnp.stack(
        (jnp.stack((rows_0[0], side_0)), jnp.stack((rows_1[0], side_1)))
    )
    weight_rows = jnp.stack((own_rows, other_rows))
    weighted = (weight_rows[..., None] * tan_rows).astype(jnp.bfloat16)
    block = down_0.shape[0]
    parts = [weighted[..., :block]]
    for k in range(1, 4):
        parts.append(fetch_d(weighted[..., k * block : (k + 1) * block], kx=k))
    w_pair = jnp.stack(parts, axis=1)
    w_pair = w_pair.transpose(2, 0, 1, 3, 4)
    lo_1, hi_1 = far_x(after(one_1, w_pair), after(three_1, w_pair))
    hidden_all = jnp.concatenate((hid_0, one_0, lo_0, hi_0, three_0, hid_1, one_1, lo_1, hi_1, three_1))
    hidden_all = hidden_all.reshape(-1, hid_0.shape[-1])

    w_one, w_three, halves = gather_y(w_pair)
    gathered = []
    own = (w_pair, w_one, w_three, jnp.concatenate(halves))
    for parts in (own, [fetch_t(part, kc=1) for part in own]):
        gathered.append(jnp.stack([part.transpose(1, 2, 0, 3, 4) for part in parts], axis=2))
    weighted_all = jnp.stack(gathered, axis=2).reshape(-1, block)
    curvature = lax.dot_general(
        weighted_all, hidden_all, (((0,), (0,)), ((), ())), preferred_element_type=jnp.float32
    )
    curvature = curvature.astype(jnp.bfloat16).T

    others = fetch_d(after(rows_1.astype(jnp.bfloat16), w_pair), kh=1)
    out_tangent, layer_out = whole_rows(rows_0.astype(jnp.bfloat16), others, place_h, place_x)
    return layer_out, out_tangent, curvature


def solution(mesh):
    placed = (
        P(("dp", "tensor"), None),
        P(("dp", "tensor"), None),
        P("dp"),
        P(None, "tensor"),
        P(None, "tensor"),
        P("tensor", "dp"),
    )
    return jax.shard_map(
        shards,
        mesh=mesh,
        in_specs=placed,
        out_specs=(P(("dp", "tensor"), None), P(("dp", "tensor"), None), P("tensor", "dp")),
        check_vma=False,
    )
```

```python
import jax
import jax.numpy as jnp
from jax import lax
from jax.experimental import pallas as pl
from jax.experimental.pallas import tpu as pltpu
from jax.sharding import PartitionSpec as P

gelu_scale = 0.7978845608
cubic_coeff = 0.044715


def fetch_t(value, ky=0, kz=0, kc=0):
    key = ky * 4 + kz * 2 + kc
    return lax.ppermute(value, "tensor", [(i ^ key, i) for i in range(16)])


def fetch_d(value, kh=0, kx=0):
    key = kh * 4 + kx
    return lax.ppermute(value, "dp", [(i ^ key, i) for i in range(8)])


def after(value, *done):
    def nothing(*refs):
        del refs

    anywhere = pl.BlockSpec(memory_space=pl.ANY)
    return pl.pallas_call(
        nothing,
        out_shape=jax.ShapeDtypeStruct(value.shape, value.dtype),
        in_specs=[anywhere] * (1 + len(done)),
        out_specs=anywhere,
        input_output_aliases={0: 0},
        compiler_params=pltpu.CompilerParams(vmem_limit_bytes=1 << 17),
    )(value, *done)


def exchange_x(value):
    return fetch_d(value, kx=1), fetch_d(value, kx=3)


def far_x(one, three):
    half = one.shape[0] // 2
    return fetch_d(three[:half], kx=1), fetch_d(one[half:], kx=3)


def gather_y(pair):
    one = fetch_t(pair, ky=1)
    three = fetch_t(pair, ky=3)
    return one, three, (fetch_t(three[:1], ky=1), fetch_t(one[1:], ky=3))


def core_sum(partial):
    other = fetch_t(partial[:, 1], kc=1)
    return partial[:, 0].astype(jnp.float32) + other.astype(jnp.float32)


def column_sum(chip, ready=()):
    column = after(chip[:, 0], *ready) if ready else chip[:, 0]
    for key, place in ((2, 3), (1, 1), (3, 2)):
        got = fetch_t(chip[:, place].astype(jnp.bfloat16), ky=key)
        column = column + got.astype(jnp.float32)
    return column


def side_sum(column):
    high, groups = column.shape[:2]
    send = jnp.concatenate((column[:, :, 1], column[:, :1, 0]), axis=1).astype(jnp.bfloat16)
    got = fetch_t(send, kz=1).astype(jnp.float32)
    return column[:, :, 0] + got[:, :groups], column[:, 0, 1] + got[:, groups]


def gelu_pair(values_in):
    inner_arg = gelu_scale * (values_in + cubic_coeff * values_in * values_in * values_in)
    tanh_term = jnp.tanh(inner_arg)
    activated = 0.5 * values_in * (1.0 + tanh_term)
    gelu_slope = 0.5 * (1.0 + tanh_term) + 0.5 * values_in * (
        1.0 - tanh_term * tanh_term
    ) * gelu_scale * (1.0 + 3.0 * cubic_coeff * values_in * values_in)
    return (activated, gelu_slope)


def gate_of(own, other, gate_weight):
    flat = jnp.concatenate((*own, *other))
    flat = flat.reshape(-1, flat.shape[-1])
    return flat, jnp.dot(flat, gate_weight, preferred_element_type=jnp.float32)


def hidden_of(flat, gate, up_weight, rows):
    up = jnp.dot(flat, up_weight, preferred_element_type=jnp.float32)
    gate = gate.reshape(-1, 2, rows, gate.shape[1])
    up = up.reshape(-1, 2, rows, up.shape[1])
    activated, gelu_slope = gelu_pair(gate[:, 0])
    hidden = activated * up[:, 0]
    tangent = gelu_slope * gate[:, 1] * up[:, 0] + activated * up[:, 1]
    both = jnp.stack((tangent.astype(jnp.bfloat16), hidden.astype(jnp.bfloat16)))
    return both.reshape(2, 2, -1, gate.shape[-1])


def product(left, blocks, rows):
    groups = left.shape[0]
    left = left.reshape(-1, left.shape[-1])
    height, depth = left.shape
    columns = sum(block.shape[0] for block in blocks)
    tile = 256 if columns % 256 == 0 else columns
    n_block = len(blocks)

    def kernel(left_ref, *refs):
        out_ref, right_ref, sems = refs[-3:]
        copies, place = [], 0
        for k, block in enumerate(refs[:n_block]):
            size = block.shape[0]
            copy = pltpu.make_async_copy(block, right_ref.at[pl.ds(place, size)], sems.at[k])
            copy.start()
            copies.append((place, copy))
            place += size
        for at in range(0, columns, tile):
            while copies and copies[0][0] < at + tile:
                copies.pop(0)[1].wait()
            total = lax.dot_general(
                left_ref[...],
                right_ref[at : at + tile, :],
                (((1,), (1,)), ((), ())),
                preferred_element_type=jnp.float32,
            )
            out_ref[:, at : at + tile] = total.astype(jnp.bfloat16)

    near = pl.BlockSpec(memory_space=pltpu.VMEM)
    anywhere = pl.BlockSpec(memory_space=pl.ANY)
    out = pl.pallas_call(
        kernel,
        out_shape=jax.ShapeDtypeStruct((height, columns), jnp.bfloat16),
        in_specs=[near] + [anywhere] * n_block,
        out_specs=near,
        scratch_shapes=[
            pltpu.VMEM((columns, depth), jnp.bfloat16),
            pltpu.SemaphoreType.DMA((n_block,)),
        ],
        compiler_params=pltpu.CompilerParams(vmem_limit_bytes=16 << 20),
        cost_estimate=pl.CostEstimate(
            flops=2 * height * depth * columns,
            bytes_accessed=2 * columns * (depth + height),
            transcendentals=0,
        ),
    )(left, *blocks)
    return out.reshape(groups, 2, 4, 2, rows, columns)


def whole_rows(own, other, place_h, place_x):
    block = own.shape[-1] // 4
    both = jnp.stack((own, other))
    b = [both[..., k * block : (k + 1) * block] for k in range(4)]
    odd = place_x & 1 == 1
    one = [jnp.where(odd, b[k ^ 1], b[k]) for k in range(4)]
    high = place_x & 2 == 2
    two = [jnp.where(high, one[k ^ 2], one[k]) for k in range(4)]
    second = place_h == 1
    halves = [[jnp.where(second, t[1 - h], t[h]) for t in two] for h in range(2)]
    return jnp.concatenate(halves[0] + halves[1], axis=-1)


def shards(tokens, tangent, hessian_weight, gate_weight, up_weight, down_weight):
    rows, width = tokens.shape
    place_d = lax.axis_index("dp")
    place_t = lax.axis_index("tensor")
    place_h, place_x = place_d // 4, place_d % 4

    piece = jnp.stack((tokens, tangent))
    pair = jnp.stack((piece, fetch_t(piece, kz=1)))
    pair_other = fetch_t(pair, kc=1)
    one, three, halves = gather_y(pair)
    one_other = fetch_t(one, kc=1)
    three_other = fetch_t(three, kc=1)

    down_0 = after(down_weight.T, piece)
    down_1, down_3 = exchange_x(down_0)
    down_lo, down_hi = far_x(down_1, down_3)
    down_half = (down_0, down_1, down_lo, down_hi, down_3)

    own_rows = jnp.stack(
        [
            lax.dynamic_slice_in_dim(hessian_weight, (place_t ^ key) * rows, rows, 0)
            for key in (0, 2)
        ]
    )
    other_rows = fetch_d(after(own_rows, pair), kh=1)

    pair_other = after(pair_other, other_rows)
    flat, gate = gate_of((pair, one), (pair_other, one_other), gate_weight)
    two = jnp.concatenate([after(half, gate) for half in halves])
    two_other = fetch_t(two, kc=1)
    both_a = hidden_of(after(flat, gate, down_1, down_3), gate, up_weight, rows)
    both_a1 = fetch_d(both_a, kh=1)
    two_other = after(two_other, both_a)
    both_b = hidden_of(
        *gate_of((three, two), (three_other, two_other), gate_weight), up_weight, rows
    )
    both_b1 = fetch_d(both_b, kh=1)
    both_0 = jnp.concatenate((both_a, both_b), axis=2)
    both_1 = jnp.concatenate((both_a1, both_b1), axis=2)

    hid_0, hid_1 = both_0[1], both_1[1]
    one_0, three_0 = exchange_x(hid_0)
    chip_0 = core_sum(product(after(both_0, both_a1), down_half, rows))
    partial_1 = product(after(both_1, chip_0, one_0, three_0), down_half, rows)
    column_0 = column_sum(chip_0, (partial_1,))
    chip_1 = core_sum(partial_1)
    one_1, three_1 = exchange_x(after(hid_1, column_0))
    column_1 = column_sum(chip_1, (one_1, three_1))
    three_0, one_1 = after(three_0, column_1), after(one_1, column_1)
    two_0 = fetch_d(three_0, kx=1)
    two_1 = fetch_d(one_1, kx=3)
    own_sums, side_sums = side_sum(jnp.stack((column_0, column_1)))

    tan_rows = jnp.stack((own_sums[:, 0], side_sums), axis=1)
    weight_rows = jnp.stack((own_rows, other_rows))
    weighted = (weight_rows[..., None] * tan_rows).astype(jnp.bfloat16)
    weighted = after(weighted, two_0, two_1)
    block = down_0.shape[0]
    parts = [weighted[..., :block]]
    for k in range(1, 4):
        parts.append(fetch_d(weighted[..., k * block : (k + 1) * block], kx=k))
    w_pair = jnp.stack(parts, axis=1)
    w_pair = w_pair.transpose(2, 0, 1, 3, 4)
    hidden_all = jnp.concatenate(
        (hid_0, one_0, two_0, three_0, hid_1, one_1, two_1, three_1)
    ).reshape(-1, hid_0.shape[-1])

    w_one, w_three, halves = gather_y(w_pair)
    gathered = []
    own = (w_pair, w_one, w_three, jnp.concatenate(halves))
    for parts in (own, [fetch_t(part, kc=1) for part in own]):
        gathered.append(jnp.stack([part.transpose(1, 2, 0, 3, 4) for part in parts], axis=2))
    weighted_all = jnp.stack(gathered, axis=2).reshape(-1, block)
    curvature = lax.dot_general(
        weighted_all, hidden_all, (((0,), (0,)), ((), ())), preferred_element_type=jnp.float32
    )
    curvature = curvature.astype(jnp.bfloat16).T

    sums = own_sums.astype(jnp.bfloat16)
    others = fetch_d(sums[1], kh=1)
    out_tangent, layer_out = whole_rows(after(sums[0], w_pair), others, place_h, place_x)
    return layer_out, out_tangent, curvature


def solution(mesh):
    placed = (
        P(("dp", "tensor"), None),
        P(("dp", "tensor"), None),
        P("dp"),
        P(None, "tensor"),
        P(None, "tensor"),
        P("tensor", "dp"),
    )
    return jax.shard_map(
        shards,
        mesh=mesh,
        in_specs=placed,
        out_specs=(P(("dp", "tensor"), None), P(("dp", "tensor"), None), P("tensor", "dp")),
        check_vma=False,
    )
```

```python
import jax
import jax.numpy as jnp
from jax import lax
from jax.experimental import pallas as pl
from jax.experimental.pallas import tpu as pltpu
from jax.sharding import PartitionSpec as P

gelu_scale = 0.7978845608
cubic_coeff = 0.044715


def fetch_t(value, ky=0, kz=0, kc=0):
    key = ky * 4 + kz * 2 + kc
    return lax.ppermute(value, "tensor", [(i ^ key, i) for i in range(16)])


def fetch_d(value, kh=0, kx=0):
    key = kh * 4 + kx
    return lax.ppermute(value, "dp", [(i ^ key, i) for i in range(8)])


def after(value, *done):
    def nothing(*refs):
        del refs

    anywhere = pl.BlockSpec(memory_space=pl.ANY)
    return pl.pallas_call(
        nothing,
        out_shape=jax.ShapeDtypeStruct(value.shape, value.dtype),
        in_specs=[anywhere] * (1 + len(done)),
        out_specs=anywhere,
        input_output_aliases={0: 0},
        compiler_params=pltpu.CompilerParams(vmem_limit_bytes=1 << 17),
    )(value, *done)


def exchange_x(value):
    return fetch_d(value, kx=1), fetch_d(value, kx=3)


def far_x(one, three):
    half = one.shape[0] // 2
    return fetch_d(three[:half], kx=1), fetch_d(one[half:], kx=3)


def gather_y(pair):
    one = fetch_t(pair, ky=1)
    three = fetch_t(pair, ky=3)
    return one, three, (fetch_t(three[:1], ky=1), fetch_t(one[1:], ky=3))


def core_sum(partial):
    other = fetch_t(partial[:, 1], kc=1)
    return partial[:, 0].astype(jnp.float32) + other.astype(jnp.float32)


def column_sum(chip, ready=()):
    column = after(chip[:, 0], *ready) if ready else chip[:, 0]
    for key, place in ((2, 3), (1, 1), (3, 2)):
        got = fetch_t(chip[:, place].astype(jnp.bfloat16), ky=key)
        column = column + got.astype(jnp.float32)
    return column


def side_sum(column):
    first = fetch_t(column[:, 0, ::-1].astype(jnp.bfloat16), kz=1)
    second = fetch_t(column[:, 1, 1].astype(jnp.bfloat16), kz=1)
    return (
        column[:, 0] + first.astype(jnp.float32),
        column[:, 1, 0] + second.astype(jnp.float32),
    )


def gelu_pair(values_in):
    inner_arg = gelu_scale * (values_in + cubic_coeff * values_in * values_in * values_in)
    tanh_term = jnp.tanh(inner_arg)
    activated = 0.5 * values_in * (1.0 + tanh_term)
    gelu_slope = 0.5 * (1.0 + tanh_term) + 0.5 * values_in * (
        1.0 - tanh_term * tanh_term
    ) * gelu_scale * (1.0 + 3.0 * cubic_coeff * values_in * values_in)
    return (activated, gelu_slope)


def gate_of(own, other, gate_weight):
    flat = jnp.concatenate((*own, *other))
    flat = flat.reshape(-1, flat.shape[-1])
    return flat, jnp.dot(flat, gate_weight, preferred_element_type=jnp.float32)


def hidden_of(flat, gate, up_weight, rows):
    up = jnp.dot(flat, up_weight, preferred_element_type=jnp.float32)
    gate = gate.reshape(-1, 2, rows, gate.shape[1])
    up = up.reshape(-1, 2, rows, up.shape[1])
    activated, gelu_slope = gelu_pair(gate[:, 0])
    hidden = activated * up[:, 0]
    tangent = gelu_slope * gate[:, 1] * up[:, 0] + activated * up[:, 1]
    both = jnp.stack((tangent.astype(jnp.bfloat16), hidden.astype(jnp.bfloat16)))
    return both.reshape(2, 2, -1, gate.shape[-1])


def product(left, blocks, rows):
    groups = left.shape[0]
    left = left.reshape(-1, left.shape[-1])
    height, depth = left.shape
    columns = sum(block.shape[0] for block in blocks)
    tile = 256 if columns % 256 == 0 else columns
    n_block = len(blocks)

    def kernel(left_ref, *refs):
        out_ref, right_ref, sems = refs[-3:]
        copies, place = [], 0
        for k, block in enumerate(refs[:n_block]):
            size = block.shape[0]
            copy = pltpu.make_async_copy(block, right_ref.at[pl.ds(place, size)], sems.at[k])
            copy.start()
            copies.append((place, copy))
            place += size
        for at in range(0, columns, tile):
            while copies and copies[0][0] < at + tile:
                copies.pop(0)[1].wait()
            total = lax.dot_general(
                left_ref[...],
                right_ref[at : at + tile, :],
                (((1,), (1,)), ((), ())),
                preferred_element_type=jnp.float32,
            )
            out_ref[:, at : at + tile] = total.astype(jnp.bfloat16)

    near = pl.BlockSpec(memory_space=pltpu.VMEM)
    anywhere = pl.BlockSpec(memory_space=pl.ANY)
    out = pl.pallas_call(
        kernel,
        out_shape=jax.ShapeDtypeStruct((height, columns), jnp.bfloat16),
        in_specs=[near] + [anywhere] * n_block,
        out_specs=near,
        scratch_shapes=[
            pltpu.VMEM((columns, depth), jnp.bfloat16),
            pltpu.SemaphoreType.DMA((n_block,)),
        ],
        compiler_params=pltpu.CompilerParams(vmem_limit_bytes=16 << 20),
        cost_estimate=pl.CostEstimate(
            flops=2 * height * depth * columns,
            bytes_accessed=2 * columns * (depth + height),
            transcendentals=0,
        ),
    )(left, *blocks)
    return out.reshape(groups, 2, 4, 2, rows, columns)


def outer_sum(weighted, blocks):
    blocks = [block.reshape(-1, block.shape[-1]) for block in blocks]
    tokens, columns = weighted.shape
    width = blocks[0].shape[1]
    tile = 384 if width % 384 == 0 else width
    n_block = len(blocks)

    def kernel(weighted_ref, *refs):
        out_ref, hidden_ref, sems = refs[-3:]
        copies, place = [], 0
        for k, block in enumerate(refs[:n_block]):
            size = block.shape[0]
            copies.append(
                pltpu.make_async_copy(block, hidden_ref.at[pl.ds(place, size)], sems.at[k])
            )
            copies[-1].start()
            place += size
        for copy in copies:
            copy.wait()
        for at in range(0, width, tile):
            total = lax.dot_general(
                weighted_ref[...],
                hidden_ref[:, at : at + tile],
                (((0,), (0,)), ((), ())),
                preferred_element_type=jnp.float32,
            )
            out_ref[:, at : at + tile] = total.astype(jnp.bfloat16)

    near = pl.BlockSpec(memory_space=pltpu.VMEM)
    anywhere = pl.BlockSpec(memory_space=pl.ANY)
    return pl.pallas_call(
        kernel,
        out_shape=jax.ShapeDtypeStruct((columns, width), jnp.bfloat16),
        in_specs=[near] + [anywhere] * n_block,
        out_specs=near,
        scratch_shapes=[
            pltpu.VMEM((tokens, width), jnp.bfloat16),
            pltpu.SemaphoreType.DMA((n_block,)),
        ],
        compiler_params=pltpu.CompilerParams(vmem_limit_bytes=20 << 20),
        cost_estimate=pl.CostEstimate(
            flops=2 * tokens * columns * width,
            bytes_accessed=2 * (tokens * (columns + width) + columns * width),
            transcendentals=0,
        ),
    )(weighted, *blocks)


def whole_rows(own, other, place_h, place_x):
    block = own.shape[-1] // 4
    both = jnp.stack((own, other))
    b = [both[..., k * block : (k + 1) * block] for k in range(4)]
    odd = place_x & 1 == 1
    one = [jnp.where(odd, b[k ^ 1], b[k]) for k in range(4)]
    high = place_x & 2 == 2
    two = [jnp.where(high, one[k ^ 2], one[k]) for k in range(4)]
    second = place_h == 1
    halves = [[jnp.where(second, t[1 - h], t[h]) for t in two] for h in range(2)]
    return jnp.concatenate(halves[0] + halves[1], axis=-1)


def shards(tokens, tangent, hessian_weight, gate_weight, up_weight, down_weight):
    rows, width = tokens.shape
    place_d = lax.axis_index("dp")
    place_t = lax.axis_index("tensor")
    place_h, place_x = place_d // 4, place_d % 4

    piece = jnp.stack((tokens, tangent))
    pair = jnp.stack((piece, fetch_t(piece, kz=1)))
    pair_other = fetch_t(pair, kc=1)
    one, three, halves = gather_y(pair)
    one_other = fetch_t(one, kc=1)
    three_other = fetch_t(three, kc=1)

    down_0 = after(down_weight.T, piece)
    down_1, down_3 = exchange_x(down_0)
    down_lo, down_hi = far_x(down_1, down_3)
    down_half = (down_0, down_1, down_lo, down_hi, down_3)

    own_rows = jnp.stack(
        [
            lax.dynamic_slice_in_dim(hessian_weight, (place_t ^ key) * rows, rows, 0)
            for key in (0, 2)
        ]
    )

    flat, gate = gate_of((pair, one), (pair_other, one_other), gate_weight)
    two = jnp.concatenate([after(half, gate) for half in halves])
    two_other = fetch_t(two, kc=1)
    both_a = hidden_of(after(flat, gate, down_1, down_3), gate, up_weight, rows)
    both_a1 = fetch_d(both_a, kh=1)
    other_rows = fetch_d(after(own_rows, both_a), kh=1)
    two_other = after(two_other, both_a)
    both_b = hidden_of(
        *gate_of((three, two), (three_other, two_other), gate_weight), up_weight, rows
    )
    both_b1 = fetch_d(both_b, kh=1)
    both_0 = jnp.concatenate((both_a, both_b), axis=2)
    both_1 = jnp.concatenate((both_a1, both_b1), axis=2)

    hid_0, hid_1 = both_0[1], both_1[1]
    one_0, three_0 = exchange_x(hid_0)
    chip_0 = core_sum(product(after(both_0, both_a1, other_rows), down_half, rows))
    partial_1 = product(after(both_1, chip_0, one_0, three_0), down_half, rows)
    column_0 = column_sum(chip_0, (partial_1,))
    chip_1 = core_sum(partial_1)
    one_1, three_1 = exchange_x(after(hid_1, column_0))
    column_1 = column_sum(chip_1, (one_1, three_1))
    tan_rows, out_rows = side_sum(jnp.stack((column_0, column_1)))

    weight_rows = jnp.stack((own_rows, other_rows))
    weighted = (weight_rows[..., None] * tan_rows).astype(jnp.bfloat16)
    block = down_0.shape[0]
    parts = [weighted[..., :block]]
    for k in range(1, 4):
        parts.append(fetch_d(weighted[..., k * block : (k + 1) * block], kx=k))
    w_pair = jnp.stack(parts, axis=1)
    w_pair = w_pair.transpose(2, 0, 1, 3, 4)
    three_0, one_1 = after(three_0, w_pair), after(one_1, w_pair)
    two_0 = fetch_d(three_0, kx=1)
    two_1 = fetch_d(one_1, kx=3)
    hidden_all = (hid_0, one_0, two_0, three_0, both_1[1], one_1, two_1, three_1)

    w_one, w_three, halves = gather_y(w_pair)
    swapped = fetch_t(w_pair, kc=1)
    gathered = []
    own = (w_pair, w_one, w_three, jnp.concatenate(halves))
    for parts in (own, [swapped] + [fetch_t(part, kc=1) for part in own[1:]]):
        gathered.append(jnp.stack([part.transpose(1, 2, 0, 3, 4) for part in parts], axis=2))
    weighted_all = jnp.stack(gathered, axis=2).reshape(-1, block)
    curvature = outer_sum(weighted_all, hidden_all).T

    sums = jnp.stack((tan_rows[:, 0], out_rows), axis=1).astype(jnp.bfloat16)
    others = fetch_d(after(sums[1], swapped), kh=1)
    out_tangent, layer_out = whole_rows(sums[0], others, place_h, place_x)
    return layer_out, out_tangent, curvature


def solution(mesh):
    placed = (
        P(("dp", "tensor"), None),
        P(("dp", "tensor"), None),
        P("dp"),
        P(None, "tensor"),
        P(None, "tensor"),
        P("tensor", "dp"),
    )
    return jax.shard_map(
        shards,
        mesh=mesh,
        in_specs=placed,
        out_specs=(P(("dp", "tensor"), None), P(("dp", "tensor"), None), P("tensor", "dp")),
        check_vma=False,
    )
```

```python
import jax
import jax.numpy as jnp
from jax import lax
from jax.experimental import pallas as pl
from jax.experimental.pallas import tpu as pltpu
from jax.sharding import PartitionSpec as P

gelu_scale = 0.7978845608
cubic_coeff = 0.044715


def fetch_t(value, ky=0, kz=0, kc=0):
    key = ky * 4 + kz * 2 + kc
    return lax.ppermute(value, "tensor", [(i ^ key, i) for i in range(16)])


def fetch_d(value, kh=0, kx=0):
    key = kh * 4 + kx
    return lax.ppermute(value, "dp", [(i ^ key, i) for i in range(8)])


def after(value, *done):
    def nothing(*refs):
        del refs

    anywhere = pl.BlockSpec(memory_space=pl.ANY)
    return pl.pallas_call(
        nothing,
        out_shape=jax.ShapeDtypeStruct(value.shape, value.dtype),
        in_specs=[anywhere] * (1 + len(done)),
        out_specs=anywhere,
        input_output_aliases={0: 0},
        compiler_params=pltpu.CompilerParams(vmem_limit_bytes=1 << 17),
    )(value, *done)


def exchange_x(value):
    return fetch_d(value, kx=1), fetch_d(value, kx=3)


def far_x(one, three):
    half = one.shape[0] // 2
    return fetch_d(three[:half], kx=1), fetch_d(one[half:], kx=3)


def gather_y(pair):
    one = fetch_t(pair, ky=1)
    three = fetch_t(pair, ky=3)
    return one, three, (fetch_t(three[:1], ky=1), fetch_t(one[1:], ky=3))


def core_sum(partial):
    other = fetch_t(partial[:, 1], kc=1)
    return partial[:, 0].astype(jnp.float32) + other.astype(jnp.float32)


def column_sum(chip, ready=()):
    column = after(chip[:, 0], *ready) if ready else chip[:, 0]
    for key, place in ((2, 3), (1, 1), (3, 2)):
        got = fetch_t(chip[:, place].astype(jnp.bfloat16), ky=key)
        column = column + got.astype(jnp.float32)
    return column


def side_sum(column):
    first = fetch_t(column[:, 0, ::-1].astype(jnp.bfloat16), kz=1)
    second = fetch_t(column[:, 1, 1].astype(jnp.bfloat16), kz=1)
    return (
        column[:, 0] + first.astype(jnp.float32),
        column[:, 1, 0] + second.astype(jnp.float32),
    )


def gelu_pair(values_in):
    inner_arg = gelu_scale * (values_in + cubic_coeff * values_in * values_in * values_in)
    tanh_term = jnp.tanh(inner_arg)
    activated = 0.5 * values_in * (1.0 + tanh_term)
    gelu_slope = 0.5 * (1.0 + tanh_term) + 0.5 * values_in * (
        1.0 - tanh_term * tanh_term
    ) * gelu_scale * (1.0 + 3.0 * cubic_coeff * values_in * values_in)
    return (activated, gelu_slope)


def gate_of(own, other, gate_weight):
    flat = jnp.concatenate((*own, *other))
    flat = flat.reshape(-1, flat.shape[-1])
    return flat, jnp.dot(flat, gate_weight, preferred_element_type=jnp.float32)


def hidden_of(flat, gate, up_weight, rows):
    up = jnp.dot(flat, up_weight, preferred_element_type=jnp.float32)
    gate = gate.reshape(-1, 2, rows, gate.shape[1])
    up = up.reshape(-1, 2, rows, up.shape[1])
    activated, gelu_slope = gelu_pair(gate[:, 0])
    hidden = activated * up[:, 0]
    tangent = gelu_slope * gate[:, 1] * up[:, 0] + activated * up[:, 1]
    both = jnp.stack((tangent.astype(jnp.bfloat16), hidden.astype(jnp.bfloat16)))
    return both.reshape(2, 2, -1, gate.shape[-1])


def product(left, blocks, rows):
    groups = left.shape[0]
    left = left.reshape(-1, left.shape[-1])
    height, depth = left.shape
    columns = sum(block.shape[0] for block in blocks)
    tile = 256 if columns % 256 == 0 else columns
    n_block = len(blocks)

    def kernel(left_ref, *refs):
        out_ref, right_ref, sems = refs[-3:]
        copies, place = [], 0
        for k, block in enumerate(refs[:n_block]):
            size = block.shape[0]
            copy = pltpu.make_async_copy(block, right_ref.at[pl.ds(place, size)], sems.at[k])
            copy.start()
            copies.append((place, copy))
            place += size
        for at in range(0, columns, tile):
            while copies and copies[0][0] < at + tile:
                copies.pop(0)[1].wait()
            total = lax.dot_general(
                left_ref[...],
                right_ref[at : at + tile, :],
                (((1,), (1,)), ((), ())),
                preferred_element_type=jnp.float32,
            )
            out_ref[:, at : at + tile] = total.astype(jnp.bfloat16)

    near = pl.BlockSpec(memory_space=pltpu.VMEM)
    anywhere = pl.BlockSpec(memory_space=pl.ANY)
    out = pl.pallas_call(
        kernel,
        out_shape=jax.ShapeDtypeStruct((height, columns), jnp.bfloat16),
        in_specs=[near] + [anywhere] * n_block,
        out_specs=near,
        scratch_shapes=[
            pltpu.VMEM((columns, depth), jnp.bfloat16),
            pltpu.SemaphoreType.DMA((n_block,)),
        ],
        compiler_params=pltpu.CompilerParams(vmem_limit_bytes=16 << 20),
        cost_estimate=pl.CostEstimate(
            flops=2 * height * depth * columns,
            bytes_accessed=2 * columns * (depth + height),
            transcendentals=0,
        ),
    )(left, *blocks)
    return out.reshape(groups, 2, 4, 2, rows, columns)


def outer_sum(parts, blocks):
    rows, columns = parts[0].shape[-2:]
    width = blocks[0].shape[-1]
    parts = [part.reshape(-1, columns) for part in parts]
    blocks = [block.reshape(-1, rows, width) for block in blocks]
    pieces, n_block = blocks[0].shape[0], len(blocks)
    tokens = pieces * n_block * rows
    size = parts[0].shape[0]
    tile = 384 if width % 384 == 0 else width

    def kernel(*refs):
        out_ref, weighted_ref, hidden_ref, sems = refs[-4:]
        copies = []
        for k, part in enumerate(refs[: len(parts)]):
            target = weighted_ref.at[pl.ds(k * size, size)]
            copies.append(pltpu.make_async_copy(part, target, sems.at[k]))
        for k, block in enumerate(refs[len(parts) : len(parts) + n_block]):
            target = hidden_ref.at[:, k]
            copies.append(pltpu.make_async_copy(block, target, sems.at[len(parts) + k]))
        for copy in copies:
            copy.start()
        for copy in copies:
            copy.wait()
        for at in range(0, width, tile):
            total = lax.dot_general(
                weighted_ref[...],
                hidden_ref[:, :, :, at : at + tile].reshape(tokens, tile),
                (((0,), (0,)), ((), ())),
                preferred_element_type=jnp.float32,
            )
            out_ref[:, at : at + tile] = total.astype(jnp.bfloat16)

    near = pl.BlockSpec(memory_space=pltpu.VMEM)
    anywhere = pl.BlockSpec(memory_space=pl.ANY)
    return pl.pallas_call(
        kernel,
        out_shape=jax.ShapeDtypeStruct((columns, width), jnp.bfloat16),
        in_specs=[anywhere] * (len(parts) + n_block),
        out_specs=near,
        scratch_shapes=[
            pltpu.VMEM((tokens, columns), jnp.bfloat16),
            pltpu.VMEM((pieces, n_block, rows, width), jnp.bfloat16),
            pltpu.SemaphoreType.DMA((len(parts) + n_block,)),
        ],
        compiler_params=pltpu.CompilerParams(vmem_limit_bytes=20 << 20),
        cost_estimate=pl.CostEstimate(
            flops=2 * tokens * columns * width,
            bytes_accessed=2 * (tokens * (columns + width) + columns * width),
            transcendentals=0,
        ),
    )(*parts, *blocks)


def whole_rows(own, other, place_h, place_x):
    block = own.shape[-1] // 4
    both = jnp.stack((own, other))
    b = [both[..., k * block : (k + 1) * block] for k in range(4)]
    odd = place_x & 1 == 1
    one = [jnp.where(odd, b[k ^ 1], b[k]) for k in range(4)]
    high = place_x & 2 == 2
    two = [jnp.where(high, one[k ^ 2], one[k]) for k in range(4)]
    second = place_h == 1
    halves = [[jnp.where(second, t[1 - h], t[h]) for t in two] for h in range(2)]
    return jnp.concatenate(halves[0] + halves[1], axis=-1)


def shards(tokens, tangent, hessian_weight, gate_weight, up_weight, down_weight):
    rows, width = tokens.shape
    place_d = lax.axis_index("dp")
    place_t = lax.axis_index("tensor")
    place_h, place_x = place_d // 4, place_d % 4

    piece = jnp.stack((tokens, tangent))
    pair = jnp.stack((piece, fetch_t(piece, kz=1)))
    pair_other = fetch_t(pair, kc=1)
    one, three, halves = gather_y(pair)
    one_other = fetch_t(one, kc=1)
    three_other = fetch_t(three, kc=1)

    down_0 = after(down_weight.T, piece)
    down_1, down_3 = exchange_x(down_0)
    down_lo, down_hi = far_x(down_1, down_3)
    down_half = (down_0, down_1, down_lo, down_hi, down_3)

    own_rows = jnp.stack(
        [
            lax.dynamic_slice_in_dim(hessian_weight, (place_t ^ key) * rows, rows, 0)
            for key in (0, 2)
        ]
    )

    flat, gate = gate_of((pair, one), (pair_other, one_other), gate_weight)
    two = jnp.concatenate([after(half, gate) for half in halves])
    two_other = fetch_t(two, kc=1)
    both_a = hidden_of(after(flat, gate, down_1, down_3), gate, up_weight, rows)
    both_a1 = fetch_d(both_a, kh=1)
    other_rows = fetch_d(after(own_rows, both_a), kh=1)
    two_other = after(two_other, both_a)
    both_b = hidden_of(
        *gate_of((three, two), (three_other, two_other), gate_weight), up_weight, rows
    )
    both_b1 = fetch_d(both_b, kh=1)
    both_0 = jnp.concatenate((both_a, both_b), axis=2)
    both_1 = jnp.concatenate((both_a1, both_b1), axis=2)

    hid_0, hid_1 = both_0[1], both_1[1]
    one_0, three_0 = exchange_x(hid_0)
    chip_0 = core_sum(product(after(both_0, both_a1, other_rows), down_half, rows))
    partial_1 = product(after(both_1, chip_0, one_0, three_0), down_half, rows)
    column_0 = column_sum(chip_0, (partial_1,))
    chip_1 = core_sum(partial_1)
    one_1, three_1 = exchange_x(after(hid_1, column_0))
    column_1 = column_sum(chip_1, (one_1, three_1))
    tan_rows, out_rows = side_sum(jnp.stack((column_0, column_1)))

    weight_rows = jnp.stack((own_rows, other_rows))
    weighted = (weight_rows[..., None] * tan_rows).astype(jnp.bfloat16)
    block = down_0.shape[0]
    parts = [weighted[..., :block]]
    for k in range(1, 4):
        parts.append(fetch_d(weighted[..., k * block : (k + 1) * block], kx=k))
    w_pair = jnp.stack(parts, axis=1)
    w_pair = w_pair.transpose(2, 0, 1, 3, 4)
    three_0, one_1 = after(three_0, w_pair), after(one_1, w_pair)
    two_0 = fetch_d(three_0, kx=1)
    two_1 = fetch_d(one_1, kx=3)
    hidden_all = (hid_0, one_0, two_0, three_0, both_1[1], one_1, two_1, three_1)

    w_one, w_three, halves = gather_y(w_pair)
    own = (w_pair, w_one, w_three, jnp.concatenate(halves))
    other = [fetch_t(part, kc=1) for part in own]
    swapped = other[0]
    blocks = [block.reshape(-1, rows, block.shape[-1]) for block in hidden_all]
    curvature = outer_sum((*own, *other), blocks).T

    sums = jnp.stack((tan_rows[:, 0], out_rows), axis=1).astype(jnp.bfloat16)
    others = fetch_d(after(sums[1], swapped), kh=1)
    out_tangent, layer_out = whole_rows(sums[0], others, place_h, place_x)
    return layer_out, out_tangent, curvature


def solution(mesh):
    placed = (
        P(("dp", "tensor"), None),
        P(("dp", "tensor"), None),
        P("dp"),
        P(None, "tensor"),
        P(None, "tensor"),
        P("tensor", "dp"),
    )
    return jax.shard_map(
        shards,
        mesh=mesh,
        in_specs=placed,
        out_specs=(P(("dp", "tensor"), None), P(("dp", "tensor"), None), P("tensor", "dp")),
        check_vma=False,
    )
```

```python
import jax
import jax.numpy as jnp
from jax import lax
from jax.experimental import pallas as pl
from jax.experimental.pallas import tpu as pltpu
from jax.sharding import PartitionSpec as P

gelu_scale = 0.7978845608
cubic_coeff = 0.044715


def fetch_t(value, ky=0, kz=0, kc=0):
    key = ky * 4 + kz * 2 + kc
    return lax.ppermute(value, "tensor", [(i ^ key, i) for i in range(16)])


def fetch_d(value, kh=0, kx=0):
    key = kh * 4 + kx
    return lax.ppermute(value, "dp", [(i ^ key, i) for i in range(8)])


def after(value, *done):
    def nothing(*refs):
        del refs

    anywhere = pl.BlockSpec(memory_space=pl.ANY)
    return pl.pallas_call(
        nothing,
        out_shape=jax.ShapeDtypeStruct(value.shape, value.dtype),
        in_specs=[anywhere] * (1 + len(done)),
        out_specs=anywhere,
        input_output_aliases={0: 0},
        compiler_params=pltpu.CompilerParams(vmem_limit_bytes=1 << 17),
    )(value, *done)


def exchange_x(value):
    return fetch_d(value, kx=1), fetch_d(value, kx=3)


def far_x(one, three):
    half = one.shape[0] // 2
    return fetch_d(three[:half], kx=1), fetch_d(one[half:], kx=3)


def gather_y(pair):
    one = fetch_t(pair, ky=1)
    three = fetch_t(pair, ky=3)
    return one, three, (fetch_t(three[:1], ky=1), fetch_t(one[1:], ky=3))


def core_sum(partial):
    other = fetch_t(partial[:, 1], kc=1)
    return partial[:, 0].astype(jnp.float32) + other.astype(jnp.float32)


def column_sum(chip, ready=()):
    column = after(chip[:, 0], *ready) if ready else chip[:, 0]
    for key, place in ((2, 3), (1, 1), (3, 2)):
        got = fetch_t(chip[:, place].astype(jnp.bfloat16), ky=key)
        column = column + got.astype(jnp.float32)
    return column


def side_sum(column):
    first = fetch_t(column[:, 0, ::-1].astype(jnp.bfloat16), kz=1)
    second = fetch_t(column[:, 1, 1].astype(jnp.bfloat16), kz=1)
    return (
        column[:, 0] + first.astype(jnp.float32),
        column[:, 1, 0] + second.astype(jnp.float32),
    )


def gelu_pair(values_in):
    inner_arg = gelu_scale * (values_in + cubic_coeff * values_in * values_in * values_in)
    tanh_term = jnp.tanh(inner_arg)
    activated = 0.5 * values_in * (1.0 + tanh_term)
    gelu_slope = 0.5 * (1.0 + tanh_term) + 0.5 * values_in * (
        1.0 - tanh_term * tanh_term
    ) * gelu_scale * (1.0 + 3.0 * cubic_coeff * values_in * values_in)
    return (activated, gelu_slope)


def gate_of(own, other, gate_weight):
    flat = jnp.concatenate((*own, *other))
    flat = flat.reshape(-1, flat.shape[-1])
    return flat, jnp.dot(flat, gate_weight, preferred_element_type=jnp.float32)


def hidden_of(flat, gate, up_weight, rows):
    up = jnp.dot(flat, up_weight, preferred_element_type=jnp.float32)
    gate = gate.reshape(-1, 2, rows, gate.shape[1])
    up = up.reshape(-1, 2, rows, up.shape[1])
    activated, gelu_slope = gelu_pair(gate[:, 0])
    hidden = activated * up[:, 0]
    tangent = gelu_slope * gate[:, 1] * up[:, 0] + activated * up[:, 1]
    both = jnp.stack((tangent.astype(jnp.bfloat16), hidden.astype(jnp.bfloat16)))
    return both.reshape(2, 2, -1, gate.shape[-1])


def product(left, blocks, rows):
    groups = left.shape[0]
    left = left.reshape(-1, left.shape[-1])
    height, depth = left.shape
    columns = sum(block.shape[0] for block in blocks)
    tile = 256 if columns % 256 == 0 else columns
    n_block = len(blocks)

    def kernel(left_ref, *refs):
        out_ref, right_ref, sems = refs[-3:]
        copies, place = [], 0
        for k, block in enumerate(refs[:n_block]):
            size = block.shape[0]
            copy = pltpu.make_async_copy(block, right_ref.at[pl.ds(place, size)], sems.at[k])
            copy.start()
            copies.append((place, copy))
            place += size
        for at in range(0, columns, tile):
            while copies and copies[0][0] < at + tile:
                copies.pop(0)[1].wait()
            total = lax.dot_general(
                left_ref[...],
                right_ref[at : at + tile, :],
                (((1,), (1,)), ((), ())),
                preferred_element_type=jnp.float32,
            )
            out_ref[:, at : at + tile] = total.astype(jnp.bfloat16)

    near = pl.BlockSpec(memory_space=pltpu.VMEM)
    anywhere = pl.BlockSpec(memory_space=pl.ANY)
    out = pl.pallas_call(
        kernel,
        out_shape=jax.ShapeDtypeStruct((height, columns), jnp.bfloat16),
        in_specs=[near] + [anywhere] * n_block,
        out_specs=near,
        scratch_shapes=[
            pltpu.VMEM((columns, depth), jnp.bfloat16),
            pltpu.SemaphoreType.DMA((n_block,)),
        ],
        compiler_params=pltpu.CompilerParams(vmem_limit_bytes=16 << 20),
        cost_estimate=pl.CostEstimate(
            flops=2 * height * depth * columns,
            bytes_accessed=2 * columns * (depth + height),
            transcendentals=0,
        ),
    )(left, *blocks)
    return out.reshape(groups, 2, 4, 2, rows, columns)


def outer_sum(parts, blocks):
    rows, columns = parts[0].shape[-2:]
    width = blocks[0].shape[-1]
    parts = [part.reshape(-1, columns) for part in parts]
    blocks = [block.reshape(-1, rows, width) for block in blocks]
    pieces, n_block = blocks[0].shape[0], len(blocks)
    tokens = pieces * n_block * rows
    size = parts[0].shape[0]
    tile = 384 if width % 384 == 0 else width

    def kernel(*refs):
        out_ref, weighted_ref, hidden_ref, sems = refs[-4:]
        copies = []
        for k, part in enumerate(refs[: len(parts)]):
            target = weighted_ref.at[pl.ds(k * size, size)]
            copies.append(pltpu.make_async_copy(part, target, sems.at[k]))
        for k, block in enumerate(refs[len(parts) : len(parts) + n_block]):
            target = hidden_ref.at[:, k]
            copies.append(pltpu.make_async_copy(block, target, sems.at[len(parts) + k]))
        for copy in copies:
            copy.start()
        for copy in copies:
            copy.wait()
        turned = weighted_ref[...].T
        for at in range(0, width, tile):
            total = lax.dot_general(
                turned,
                hidden_ref[:, :, :, at : at + tile].reshape(tokens, tile),
                (((1,), (0,)), ((), ())),
                preferred_element_type=jnp.float32,
            )
            out_ref[:, at : at + tile] = total.astype(jnp.bfloat16)

    near = pl.BlockSpec(memory_space=pltpu.VMEM)
    anywhere = pl.BlockSpec(memory_space=pl.ANY)
    return pl.pallas_call(
        kernel,
        out_shape=jax.ShapeDtypeStruct((columns, width), jnp.bfloat16),
        in_specs=[anywhere] * (len(parts) + n_block),
        out_specs=near,
        scratch_shapes=[
            pltpu.VMEM((tokens, columns), jnp.bfloat16),
            pltpu.VMEM((pieces, n_block, rows, width), jnp.bfloat16),
            pltpu.SemaphoreType.DMA((len(parts) + n_block,)),
        ],
        compiler_params=pltpu.CompilerParams(vmem_limit_bytes=20 << 20),
        cost_estimate=pl.CostEstimate(
            flops=2 * tokens * columns * width,
            bytes_accessed=2 * (tokens * (columns + width) + columns * width),
            transcendentals=0,
        ),
    )(*parts, *blocks)


def whole_rows(own, other, place_h, place_x):
    block = own.shape[-1] // 4
    both = jnp.stack((own, other))
    b = [both[..., k * block : (k + 1) * block] for k in range(4)]
    odd = place_x & 1 == 1
    one = [jnp.where(odd, b[k ^ 1], b[k]) for k in range(4)]
    high = place_x & 2 == 2
    two = [jnp.where(high, one[k ^ 2], one[k]) for k in range(4)]
    second = place_h == 1
    halves = [[jnp.where(second, t[1 - h], t[h]) for t in two] for h in range(2)]
    return jnp.concatenate(halves[0] + halves[1], axis=-1)


def shards(tokens, tangent, hessian_weight, gate_weight, up_weight, down_weight):
    rows, width = tokens.shape
    place_d = lax.axis_index("dp")
    place_t = lax.axis_index("tensor")
    place_h, place_x = place_d // 4, place_d % 4

    piece = jnp.stack((tokens, tangent))
    pair = jnp.stack((piece, fetch_t(piece, kz=1)))
    pair_other = fetch_t(pair, kc=1)
    one, three, halves = gather_y(pair)
    one_other = fetch_t(one, kc=1)
    three_other = fetch_t(three, kc=1)

    down_0 = after(down_weight.T, piece)
    down_1, down_3 = exchange_x(down_0)
    down_lo, down_hi = far_x(down_1, down_3)
    down_half = (down_0, down_1, down_lo, down_hi, down_3)

    own_rows = jnp.stack(
        [
            lax.dynamic_slice_in_dim(hessian_weight, (place_t ^ key) * rows, rows, 0)
            for key in (0, 2)
        ]
    )

    flat, gate = gate_of((pair, one), (pair_other, one_other), gate_weight)
    two = jnp.concatenate([after(half, gate) for half in halves])
    two_other = fetch_t(two, kc=1)
    both_a = hidden_of(after(flat, gate, down_1, down_3), gate, up_weight, rows)
    both_a1 = fetch_d(both_a, kh=1)
    other_rows = fetch_d(after(own_rows, both_a), kh=1)
    two_other = after(two_other, both_a)
    both_b = hidden_of(
        *gate_of((three, two), (three_other, two_other), gate_weight), up_weight, rows
    )
    both_b1 = fetch_d(both_b, kh=1)
    both_0 = jnp.concatenate((both_a, both_b), axis=2)
    both_1 = jnp.concatenate((both_a1, both_b1), axis=2)

    hid_0, hid_1 = both_0[1], both_1[1]
    one_0, three_0 = exchange_x(hid_0)
    chip_0 = core_sum(product(after(both_0, both_a1, other_rows), down_half, rows))
    partial_1 = product(after(both_1, chip_0, one_0, three_0), down_half, rows)
    column_0 = column_sum(chip_0, (partial_1,))
    chip_1 = core_sum(partial_1)
    one_1, three_1 = exchange_x(after(hid_1, column_0))
    column_1 = column_sum(chip_1, (one_1, three_1))
    tan_rows, out_rows = side_sum(jnp.stack((column_0, column_1)))

    weight_rows = jnp.stack((own_rows, other_rows))
    weighted = (weight_rows[..., None] * tan_rows).astype(jnp.bfloat16)
    block = down_0.shape[0]
    parts = [weighted[..., :block]]
    for k in range(1, 4):
        parts.append(fetch_d(weighted[..., k * block : (k + 1) * block], kx=k))
    w_pair = jnp.stack(parts, axis=1)
    w_pair = w_pair.transpose(2, 0, 1, 3, 4)
    three_0, one_1 = after(three_0, w_pair), after(one_1, w_pair)
    two_0 = fetch_d(three_0, kx=1)
    two_1 = fetch_d(one_1, kx=3)
    hidden_all = (hid_0, one_0, two_0, three_0, both_1[1], one_1, two_1, three_1)

    w_one, w_three, halves = gather_y(w_pair)
    own = (w_pair, w_one, w_three, jnp.concatenate(halves))
    other = [fetch_t(part, kc=1) for part in own]
    swapped = other[0]
    blocks = [block.reshape(-1, rows, block.shape[-1]) for block in hidden_all]
    curvature = outer_sum((*own, *other), blocks).T

    sums = jnp.stack((tan_rows[:, 0], out_rows), axis=1).astype(jnp.bfloat16)
    others = fetch_d(after(sums[1], swapped), kh=1)
    out_tangent, layer_out = whole_rows(sums[0], others, place_h, place_x)
    return layer_out, out_tangent, curvature


def solution(mesh):
    placed = (
        P(("dp", "tensor"), None),
        P(("dp", "tensor"), None),
        P("dp"),
        P(None, "tensor"),
        P(None, "tensor"),
        P("tensor", "dp"),
    )
    return jax.shard_map(
        shards,
        mesh=mesh,
        in_specs=placed,
        out_specs=(P(("dp", "tensor"), None), P(("dp", "tensor"), None), P("tensor", "dp")),
        check_vma=False,
    )
```
